768 devices in a mesh: grp: 12 (over z), loc: 64 (over x, y, core).
Axes of the slice: x: 4, y: 8, z: 12, core: 2. Of those that a mesh axis runs over, the one named last changes fastest.
Arguments:
- tokens: bfloat16 [1536, 7168], P('grp', 'loc'), may hold values from -6 to 6
- expert_ids: int32 [1536, 8], P('grp'), may hold values from 0 to 191, as said below
- gate_weights: float32 [1536, 8], P('grp'), may hold values from 0.05 to 1
- gate_blocks: bfloat16 [768, 1792, 256], P(('grp', 'loc')), may hold values from -0.0625 to 0.0625
- up_blocks: bfloat16 [768, 1792, 256], P(('grp', 'loc')), may hold values from -0.0625 to 0.0625
- down_blocks: bfloat16 [768, 256, 1792], P(('grp', 'loc')), may hold values from -0.125 to 0.125
Outputs:
- combined: bfloat16 [1536, 7168], P('grp', 'loc')
The draws below stay inside these ranges and needn't reach their ends.
Inputs may be any that keep to these rules, and one draw needn't show every extreme that they name: `expert_ids`: each row names 8 different experts, all lying in at most 4 groups, where expert e lies in group e // 16.
All inputs are finite; a program needn't handle non-finite values.
Results may differ from the reference program's by a relative error of at most 0.0058.
Values may be sent and summed in bfloat16 or wider, within the bound.
A program may use at most 32 MiB of HBM per device.

```python
import math
import jax
import jax.numpy as jnp
from jax import lax

D = 7168
FF = 2048
TOPK = 8
TOPG = 4
GRP_EXP = 16
HSPLIT = 8
TOK_GRP = 128
TOKENS = 1536
EXP_GRP = 2
DSPLIT = 4
HS = 256
DB = 1792
SUB = 28
CAP = 8
ROWS = 96
N_GRP = 12
N_LOC = 64


def draw_expert_ids(key, part):
    key = jax.random.fold_in(key, 7)
    key_group, key_bias, key_score = jax.random.split(key, 3)
    expert_total = N_GRP * GRP_EXP
    group_score = jax.random.randint(key_group, (TOKENS, N_GRP), 0, 1 << 20) * N_GRP + jnp.arange(N_GRP, dtype=jnp.int32)[None, :]
    top_groups, chosen = lax.top_k(group_score, TOPG)
    in_chosen = jnp.any(chosen[:, :, None] == jnp.arange(N_GRP, dtype=jnp.int32)[None, None, :], axis=1)
    allowed = jnp.repeat(in_chosen, GRP_EXP, axis=1)
    expert_bias = jax.random.randint(key_bias, (expert_total,), 0, 4) * 96
    expert_score = jax.random.randint(key_score, (TOKENS, expert_total), 0, 1024) + expert_bias[None, :]
    expert_score = expert_score * expert_total + jnp.arange(expert_total, dtype=jnp.int32)[None, :]
    expert_score = jnp.where(allowed, expert_score, -1 - jnp.arange(expert_total, dtype=jnp.int32)[None, :])
    top_values, picked = lax.top_k(expert_score, TOPK)
    return picked.astype(jnp.int32)


def shard_levels(stream_key, shape, cuts, least, top_value):
    gain = 1.0
    for dim, blocks in cuts:
        draws = jax.random.uniform(jax.random.fold_in(jax.random.fold_in(stream_key, 6), dim), (blocks,), jnp.float32, least / len(cuts), top_value / len(cuts))
        gain = gain * jnp.repeat(jnp.exp(draws), shape[dim] // blocks).reshape((-1,) + (1,) * (len(shape) - 1 - dim))
    return gain


def gaussian(stream_key, extent, deviation, limit, pieces=(), kind=jnp.bfloat16):
    result = deviation * jax.random.normal(stream_key, extent, jnp.float32)
    if pieces:
        result = result * shard_levels(stream_key, extent, pieces, -0.22, 0.18)
    return jnp.clip(result, -limit, limit).astype(kind)


def setup_inputs(seed: int = 0) -> dict:
    arg_keys = jax.random.split(jax.random.key(seed), 7)
    return {
        "tokens": gaussian(arg_keys[0], (TOKENS, D), 1.0, 6.0, ((0, 12), (1, 64))),
        "expert_ids": draw_expert_ids(jax.random.fold_in(arg_keys[6], 71), 0),
        "gate_weights": jnp.clip(jnp.exp(math.log(1.0) - 2.9957323 * jax.random.uniform(arg_keys[2], (TOKENS, TOPK), jnp.float32) ** shard_levels(arg_keys[2], (TOKENS, TOPK), ((0, 12),), -0.2, 0.2)), 0.05, 1.0),
        "gate_blocks": gaussian(arg_keys[3], (N_GRP * N_LOC, DB, HS), D ** -0.5, 0.0625, ((0, 768),)),
        "up_blocks": gaussian(arg_keys[4], (N_GRP * N_LOC, DB, HS), D ** -0.5, 0.0625, ((0, 768),)),
        "down_blocks": gaussian(arg_keys[5], (N_GRP * N_LOC, HS, DB), FF ** -0.5, 0.125, ((0, 768),)),
    }


def bin_layout(expert_ids, group_count, capacity, window_experts):
    expert_total = group_count * GRP_EXP
    onehot_hits = jnp.sum((expert_ids[:, :, None] == jnp.arange(expert_total, dtype=jnp.int32)[None, None, :]).astype(jnp.int32), axis=1)
    earlier = jnp.cumsum(onehot_hits, axis=0) - onehot_hits
    slot_index = jnp.take_along_axis(earlier, expert_ids, axis=1)
    within = expert_ids % GRP_EXP
    target = expert_ids // GRP_EXP
    usable = (within < window_experts) & (slot_index < capacity)
    position = (target * capacity + jnp.minimum(slot_index, capacity - 1)) * window_experts + jnp.minimum(within, window_experts - 1)
    return usable, position.astype(jnp.int32)


def group_layout(grouped_ids):
    return bin_layout(grouped_ids, N_GRP, CAP, EXP_GRP)


def run_expert(inputs):
    gate_part, up_part, down_part, rows_in = inputs
    gate_full = gate_part.transpose(2, 0, 3, 1, 4).reshape(D, FF)
    up_full = up_part.transpose(2, 0, 3, 1, 4).reshape(D, FF)
    down_full = down_part.transpose(1, 2, 3, 0, 4).reshape(FF, D)
    gate_act = jnp.dot(rows_in, gate_full, preferred_element_type=jnp.float32)
    up_act = jnp.dot(rows_in, up_full, preferred_element_type=jnp.float32)
    hidden = (jax.nn.silu(gate_act) * up_act).astype(jnp.bfloat16)
    return jnp.dot(hidden, down_full, preferred_element_type=jnp.float32).astype(jnp.bfloat16)


def reference(tokens, expert_ids, gate_weights, gate_blocks, up_blocks, down_blocks):
    window_total = N_GRP * EXP_GRP
    grouped_ids = expert_ids.reshape(N_GRP, TOK_GRP, TOPK)
    usable, position = jax.vmap(group_layout)(grouped_ids)
    source = jnp.arange(N_GRP, dtype=jnp.int32)[:, None, None]
    within = position % EXP_GRP
    slot_index = (position // EXP_GRP) % CAP
    target = position // (EXP_GRP * CAP)
    global_row = ((target * EXP_GRP + within) * N_GRP + source) * CAP + slot_index
    global_row = jnp.where(usable, global_row, window_total * ROWS).reshape(-1).astype(jnp.int32)
    token_index = jnp.broadcast_to(jnp.arange(TOKENS, dtype=jnp.int32).reshape(N_GRP, TOK_GRP, 1), (N_GRP, TOK_GRP, TOPK)).reshape(-1)
    row_table = jnp.full((window_total * ROWS,), TOKENS, dtype=jnp.int32).at[global_row].set(token_index, mode="drop")
    padded = jnp.concatenate([tokens, jnp.zeros((1, D), tokens.dtype)], axis=0)
    bin_rows = jnp.take(padded, row_table, axis=0).reshape(window_total, ROWS, D)
    gate_parts = gate_blocks.reshape(window_total, DSPLIT, HSPLIT, N_LOC, SUB, HS)
    up_parts = up_blocks.reshape(window_total, DSPLIT, HSPLIT, N_LOC, SUB, HS)
    down_parts = down_blocks.reshape(window_total, DSPLIT, HSPLIT, HS, N_LOC, SUB)
    outputs = lax.map(run_expert, (gate_parts, up_parts, down_parts, bin_rows))
    flat_out = outputs.reshape(window_total * ROWS, D)
    safe_row = jnp.minimum(global_row, window_total * ROWS - 1).reshape(TOKENS, TOPK)
    weights = jnp.where(usable.reshape(TOKENS, TOPK), gate_weights, jnp.zeros_like(gate_weights))
    combined = jnp.zeros((TOKENS, D), jnp.float32)
    for column_index in range(TOPK):
        picked_rows = jnp.take(flat_out, safe_row[:, column_index], axis=0).astype(jnp.float32)
        combined = combined + weights[:, column_index:column_index + 1] * picked_rows
    return combined.astype(jnp.bfloat16)
```

```python
import jax
import jax.numpy as jnp
from jax import lax
from jax.experimental import pallas as pl
from jax.experimental.pallas import tpu as pltpu
from jax.sharding import PartitionSpec as P

MESH = pl.DeviceIdType.MESH
BF = jnp.bfloat16
F32 = jnp.float32

GROUPS = 12
CHIPS = 32
LINE = 8
SUB = 28
CAP = 8
QUAD = 4
PART = 24


def iota(shape, dim):
    return lax.broadcasted_iota(jnp.int32, shape, dim)


def onehot(condition):
    return jnp.where(condition, 1.0, 0.0).astype(BF)


def dot(a, b):
    return jnp.dot(a, b, preferred_element_type=F32)


def dot_nt(a, b):
    return lax.dot_general(a, b, (((1,), (1,)), ((), ())), preferred_element_type=F32)


def block_transpose(v):
    lane = iota(v[0].shape, 1)
    low64 = lane < 64
    low32 = (lane & 32) == 0
    t = [None] * 4
    for a in range(2):
        t[a] = jnp.where(low64, v[a], pltpu.roll(v[a + 2], 64, 1))
        t[a + 2] = jnp.where(low64, pltpu.roll(v[a], 64, 1), v[a + 2])
    w = [None] * 4
    for a in (0, 2):
        w[a] = jnp.where(low32, t[a], pltpu.roll(t[a + 1], 32, 1))
        w[a + 1] = jnp.where(low32, pltpu.roll(t[a], 96, 1), t[a + 1])
    return w


def send(src, dst, send_sem, recv_sem, device):
    pltpu.make_async_remote_copy(
        src_ref=src,
        dst_ref=dst,
        send_sem=send_sem,
        recv_sem=recv_sem,
        device_id=device,
        device_id_type=MESH,
    ).start()


def wait_bytes(ref, sem):
    pltpu.make_async_copy(ref, ref, sem).wait()


def expert_of(b):
    return ((b >> 4) * 16 + ((b >> 3) & 1)).astype(F32)


def kernel(
    tok_ref, ids_ref, gw_ref, wg_hbm, wu_hbm, wd_hbm, out_ref,
    wg, wu, wd, wp, dp, tmat, wt, abuf, r1, pbuf, x2, actf, gs, gr, hb,
    yb, yr, cs, r3, dbuf, r4,
    wsem, a_s, a_r, p_s, p_r, f_s, f_r, g_s, g_r, h_s, h_r, y_s, y_r, c_s, c_r, d_s, d_r,
):
    z = lax.axis_index("grp")
    l = lax.axis_index("loc")
    chip = lax.div(l, 2)
    c = lax.rem(l, 2)
    other = 1 - c
    x = lax.div(chip, LINE)
    y = lax.rem(chip, LINE)
    partner = (z, 2 * chip + other)

    loads = [
        pltpu.make_async_copy(src.at[0], dst, wsem.at[i])
        for i, (src, dst) in enumerate(((wg_hbm, wg), (wu_hbm, wu), (wd_hbm, wd)))
    ]
    for copy in loads:
        copy.start()

    barrier = pltpu.get_barrier_semaphore()

    def hello_grp(k, carry):
        pl.semaphore_signal(
            barrier, inc=1, device_id=(lax.rem(z + k, GROUPS), l), device_id_type=MESH
        )
        return carry

    lax.fori_loop(1, GROUPS, hello_grp, 0)

    def hello_loc(k, carry):
        there = lax.rem(chip + k, CHIPS)
        pl.semaphore_signal(barrier, inc=1, device_id=(z, 2 * there + c), device_id_type=MESH)
        return carry

    lax.fori_loop(1, CHIPS, hello_loc, 0)
    pl.semaphore_signal(barrier, inc=1, device_id=partner, device_id_type=MESH)

    abuf[...] = jnp.zeros(abuf.shape, BF)
    ids = ids_ref[...].astype(F32)
    eye = onehot(iota((8, 8), 0) == iota((8, 8), 1))
    ids_t = dot_nt(eye, ids.astype(BF))
    bins = GROUPS * 16
    b = iota((bins, 128), 0)
    e_b = expert_of(b)
    hit = ids_t[0:1, :] == e_b
    for k in range(1, 8):
        hit = hit | (ids_t[k : k + 1, :] == e_b)
    before = onehot(iota((128, 128), 0) < iota((128, 128), 1))
    earlier = dot(onehot(hit), before)
    selector = onehot(hit & (earlier == (b & 7).astype(F32)))
    rows = dot(selector, tok_ref[...])
    abuf[:, :, 0:112] = rows.astype(BF).reshape(GROUPS, 16, 112)

    pl.semaphore_wait(barrier, GROUPS - 1 + CHIPS - 1 + 1)

    def send_a(k, carry):
        g = lax.rem(z + k, GROUPS)
        send(abuf.at[g], r1.at[z], a_s, a_r, (g, l))
        return carry

    lax.fori_loop(1, GROUPS, send_a, 0)
    r1[pl.ds(z, 1)] = abuf[pl.ds(z, 1)]

    i = iota((128, 512), 0)
    n = iota((128, 512), 1)
    match = ((n & 31) < SUB) & (i == (n >> 7) * SUB + (n & 31))
    for r in range(QUAD):
        tmat[128 * r : 128 * (r + 1), :] = onehot(match & (((n >> 5) & 3) == r))

    loads[0].wait()
    loads[1].wait()
    i = iota((128, 112), 0)
    widen = onehot(((i & 31) < SUB) & (iota((128, 112), 1) == (i >> 5) * SUB + (i & 31)))

    def widen_in(m, carry):
        src = pl.ds(pl.multiple_of(112 * m, 16), 112)
        dst = pl.ds(pl.multiple_of(128 * lax.rem(m, 4), 128), 128)
        k = lax.div(m, 4)
        wp[k, dst, 0:256] = dot(widen, wg[src, :]).astype(BF)
        wp[k, dst, 256:512] = dot(widen, wu[src, :]).astype(BF)
        return carry

    lax.fori_loop(0, 16, widen_in, 0)

    wait_bytes(r1.at[pl.ds(0, GROUPS - 1)], a_r)
    arrived = r1[...].astype(F32)
    left = []
    for j in range(2):
        mine = arrived[:, 8 * j : 8 * j + 8, :].reshape(QUAD, PART, 128)
        left.append(jnp.concatenate([mine[r] for r in range(QUAD)], axis=1))
    packed = dot(jnp.concatenate(left, axis=0).astype(BF), tmat[...])
    for j in range(2):
        for q in range(QUAD):
            pbuf[QUAD * j + q] = packed[PART * j : PART * (j + 1), 128 * q : 128 * (q + 1)].astype(BF)

    def send_p(k, carry):
        d = lax.div(k, LINE)
        there = LINE * lax.rem(x + d, 4) + lax.rem(y + lax.rem(k, LINE), LINE)
        send(
            pbuf.at[lax.div(there, 4)], x2.at[c, chip], p_s, p_r.at[d], (z, 2 * there + c)
        )
        return carry

    lax.fori_loop(1, CHIPS, send_p, 0)
    x2[pl.ds(c, 1), pl.ds(chip, 1)] = pbuf[pl.ds(lax.div(chip, 4), 1)].reshape(1, 1, PART, 128)

    e_row = expert_of(iota((128, bins), 1))
    gate = gw_ref[...]
    same = jnp.zeros((128, bins), F32)
    weight = jnp.zeros((128, bins), F32)
    for k in range(8):
        eq = ids[:, k : k + 1] == e_row
        same = jnp.where(eq, 1.0, same)
        weight = jnp.where(eq, gate[:, k : k + 1], weight)
    after = onehot(iota((128, 128), 1) < iota((128, 128), 0))
    slot = dot(after, same.astype(BF))
    weight = jnp.where(slot == (iota((128, bins), 1) & 7).astype(F32), weight, 0.0)
    high = weight.astype(BF)
    wt[0] = high
    wt[1] = (weight - high.astype(F32)).astype(BF)

    loads[2].wait()
    for m in range(16):
        first = 112 * m // 128
        off = 112 * m - 128 * first
        width = 128 if off <= 16 else 256
        i = iota((width, 128), 0)
        n = iota((width, 128), 1)
        spread = onehot(((n & 31) < SUB) & (i == off + (n >> 5) * SUB + (n & 31)))
        dp[m // 4, :, 128 * (m % 4) : 128 * (m % 4 + 1)] = dot(
            wd[:, 128 * first : 128 * first + width], spread
        ).astype(BF)

    total = jnp.zeros((4 * PART, 512), F32)
    for step in range(5):
        if step < 4:
            ch = pl.ds(LINE * lax.rem(x + 4 - step, 4), LINE)
            wait_bytes(x2.at[0, pl.ds(0, LINE - 1 if step == 0 else LINE)], p_r.at[step])
            send(x2.at[c, ch], x2.at[c, ch], f_s, f_r.at[step], partner)
        if step >= 1:
            k = lax.rem(x + 5 - step, 4)
            wait_bytes(x2.at[0, pl.ds(0, LINE)], f_r.at[step - 1])
            half = [x2[p, pl.ds(LINE * k, LINE)].astype(F32) for p in range(2)]
            cols = []
            for m in range(4):
                w = block_transpose([half[a % 2][2 * m + a // 2] for a in range(4)])
                cols.append(jnp.concatenate(w, axis=0).astype(BF))
            total = total + dot(jnp.concatenate(cols, axis=1), wp[k])
    act = total.reshape(4, PART, 512)
    actf[...] = act
    gs[...] = act.astype(BF)

    q = 2 * lax.rem(x, 2) + lax.div(y, 4)

    def mate(qq):
        there = LINE * (2 * lax.div(x, 2) + lax.div(qq, 2)) + 4 * lax.rem(qq, 2) + lax.rem(y, 4)
        return (z, 2 * there + c)

    for k in range(1, 4):
        qq = lax.rem(q + k, 4)
        send(gs.at[qq], gr.at[q], g_s, g_r, mate(qq))
    wait_bytes(gr.at[pl.ds(0, 3)], g_r)
    summed = actf[q]
    for k in range(1, 4):
        summed = summed + gr[lax.rem(q + k, 4)].astype(F32)
    gate_act = summed[:, 0:256]
    hidden = gate_act * (1.0 / (1.0 + jnp.exp(-gate_act))) * summed[:, 256:512]
    hb[q] = hidden.astype(BF)
    for k in range(1, 4):
        send(hb.at[q], hb.at[q], h_s, h_r, mate(lax.rem(q + k, 4)))
    wait_bytes(hb.at[pl.ds(0, 3)], h_r)
    hid = hb[...].astype(F32).reshape(4 * PART, 256).astype(BF)

    for step in range(4):
        k = lax.rem(x + step, 4)
        part = dot(hid, dp[k])
        for m in range(4):
            w = block_transpose(
                [part[PART * r : PART * (r + 1), 128 * m : 128 * (m + 1)] for r in range(4)]
            )
            for a in range(4):
                yb[a % 2, LINE * k + 2 * m + a // 2] = w[a].astype(BF)
        ch = pl.ds(LINE * k, LINE)
        send(yb.at[other, ch], yr.at[ch], y_s, y_r.at[step], partner)
    for step in range(4):
        k = lax.rem(x + step, 4)
        ch = pl.ds(LINE * k, LINE)
        wait_bytes(yr.at[ch], y_r.at[step])
        cs[ch] = (yb[c, ch].astype(F32) + yr[ch].astype(F32)).astype(BF)

        def send_c(o, carry, k=k):
            there = LINE * k + lax.rem(y + o, LINE)
            send(cs.at[there], r3.at[chip], c_s, c_r, (z, 2 * there + c))
            return carry

        lax.fori_loop(1 if step == 0 else 0, LINE, send_c, 0)
        if step == 0:
            r3[pl.ds(chip, 1)] = cs[pl.ds(chip, 1)]

    wait_bytes(r3.at[pl.ds(0, CHIPS - 1)], c_r)
    parts = r3[...].astype(F32).reshape(8, 4, PART, 128)
    done = parts[:, 0] + parts[:, 1] + parts[:, 2] + parts[:, 3]
    left = [
        jnp.concatenate([done[QUAD * j + qq] for qq in range(QUAD)], axis=1) for j in range(2)
    ]
    laid = dot_nt(jnp.concatenate(left, axis=0).astype(BF), tmat[...])
    for s in range(GROUPS):
        r, k = s // 3, s % 3
        dbuf[s] = jnp.concatenate(
            [
                laid[PART * j + 8 * k : PART * j + 8 * k + 8, 128 * r : 128 * (r + 1)]
                for j in range(2)
            ],
            axis=0,
        ).astype(BF)

    def send_d(k, carry):
        s = lax.rem(z + k, GROUPS)
        send(dbuf.at[s], r4.at[z], d_s, d_r, (s, l))
        return carry

    lax.fori_loop(1, GROUPS, send_d, 0)
    r4[pl.ds(z, 1)] = dbuf[pl.ds(z, 1)]
    wait_bytes(r4.at[pl.ds(0, GROUPS - 1)], d_r)
    back = r4[...].reshape(bins, 128)
    combined = dot(wt[0], back) + dot(wt[1], back)
    out_ref[...] = combined[:, 0:112].astype(BF)

    wait_bytes(abuf.at[pl.ds(0, GROUPS - 1)], a_s)
    wait_bytes(x2.at[0, pl.ds(0, CHIPS - 1)], p_s)
    wait_bytes(x2.at[0], f_s)
    wait_bytes(gs.at[pl.ds(0, 3)], g_s)
    wait_bytes(hb.at[pl.ds(0, 3)], h_s)
    wait_bytes(yr, y_s)
    wait_bytes(cs.at[pl.ds(0, CHIPS - 1)], c_s)
    wait_bytes(dbuf.at[pl.ds(0, GROUPS - 1)], d_s)


def shards(tokens, expert_ids, gate_weights, gate_blocks, up_blocks, down_blocks):
    vmem = pl.BlockSpec(memory_space=pltpu.VMEM)
    hbm = pl.BlockSpec(memory_space=pl.ANY)
    dma = pltpu.SemaphoreType.DMA
    return pl.pallas_call(
        kernel,
        out_shape=jax.ShapeDtypeStruct(tokens.shape, BF),
        in_specs=[vmem, vmem, vmem, hbm, hbm, hbm],
        out_specs=vmem,
        scratch_shapes=[
            pltpu.VMEM((1792, 256), BF),
            pltpu.VMEM((1792, 256), BF),
            pltpu.VMEM((256, 1792), BF),
            pltpu.VMEM((4, 512, 512), BF),
            pltpu.VMEM((4, 256, 512), BF),
            pltpu.VMEM((512, 512), BF),
            pltpu.VMEM((2, 128, 192), BF),
            pltpu.VMEM((GROUPS, 16, 128), BF),
            pltpu.VMEM((GROUPS, 16, 128), BF),
            pltpu.VMEM((8, PART, 128), BF),
            pltpu.VMEM((2, CHIPS, PART, 128), BF),
            pltpu.VMEM((4, PART, 512), F32),
            pltpu.VMEM((4, PART, 512), BF),
            pltpu.VMEM((4, PART, 512), BF),
            pltpu.VMEM((4, PART, 256), BF),
            pltpu.VMEM((2, CHIPS, PART, 128), BF),
            pltpu.VMEM((CHIPS, PART, 128), BF),
            pltpu.VMEM((CHIPS, PART, 128), BF),
            pltpu.VMEM((CHIPS, PART, 128), BF),
            pltpu.VMEM((GROUPS, 16, 128), BF),
            pltpu.VMEM((GROUPS, 16, 128), BF),
            dma((3,)),
            dma, dma,
            dma, dma((4,)),
            dma, dma((4,)),
            dma, dma,
            dma, dma,
            dma, dma((4,)),
            dma, dma,
            dma, dma,
        ],
        compiler_params=pltpu.CompilerParams(
            collective_id=0, has_side_effects=True, vmem_limit_bytes=40 * 1024 * 1024
        ),
        name="moe_layer",
    )(tokens, expert_ids, gate_weights, gate_blocks, up_blocks, down_blocks)


def solution(mesh):
    in_specs = (
        P("grp", "loc"),
        P("grp", None),
        P("grp", None),
        P(("grp", "loc"), None, None),
        P(("grp", "loc"), None, None),
        P(("grp", "loc"), None, None),
    )
    return jax.shard_map(
        shards, mesh=mesh, in_specs=in_specs, out_specs=P("grp", "loc"), check_vma=False
    )
```

```python
import jax
import jax.numpy as jnp
from jax import lax
from jax.experimental import pallas as pl
from jax.experimental.pallas import tpu as pltpu
from jax.sharding import PartitionSpec as P

MESH = pl.DeviceIdType.MESH
BF = jnp.bfloat16
F32 = jnp.float32

GROUPS = 12
CHIPS = 32
LINE = 8
SUB = 28
QUAD = 4
BINS = GROUPS * 16
CHUNKS = ((0, 1), (1, 1), (2, 1))


def iota(shape, dim):
    return lax.broadcasted_iota(jnp.int32, shape, dim)


def onehot(condition):
    return jnp.where(condition, 1.0, 0.0).astype(BF)


def dot(a, b, dims=((1,), (0,))):
    return lax.dot_general(a, b, (dims, ((), ())), preferred_element_type=F32)


def offset(n):
    return lax.div(n + 1, 2) * (1 - 2 * lax.rem(n + 1, 2))


def block_transpose(v):
    lane = iota(v[0].shape, 1)
    low64 = lane < 64
    low32 = (lane & 32) == 0
    t = [None] * 4
    for a in range(2):
        t[a] = jnp.where(low64, v[a], pltpu.roll(v[a + 2], 64, 1))
        t[a + 2] = jnp.where(low64, pltpu.roll(v[a], 64, 1), v[a + 2])
    w = [None] * 4
    for a in (0, 2):
        w[a] = jnp.where(low32, t[a], pltpu.roll(t[a + 1], 32, 1))
        w[a + 1] = jnp.where(low32, pltpu.roll(t[a], 96, 1), t[a + 1])
    return w


def send(src, dst, send_sem, recv_sem, device):
    pltpu.make_async_remote_copy(
        src_ref=src,
        dst_ref=dst,
        send_sem=send_sem,
        recv_sem=recv_sem,
        device_id=device,
        device_id_type=MESH,
    ).start()


def wait_bytes(ref, sem):
    pltpu.make_async_copy(ref, ref, sem).wait()


def kernel(
    tok_hbm, ids_hbm, gw_hbm, wg_hbm, wu_hbm, wd_hbm, out_ref,
    tok, ids_v, gw, wg, wu, wd, wp, dp, tmat, wt, abuf, r1, dbuf, r4, chunk_bufs,
    load_sem, a_s, a_r, d_s, d_r, chunk_s, chunk_r,
):
    z = lax.axis_index("grp")
    l = lax.axis_index("loc")
    chip = lax.div(l, 2)
    c = lax.rem(l, 2)
    other = 1 - c
    x = lax.div(chip, LINE)
    y = lax.rem(chip, LINE)
    partner = (z, 2 * chip + other)

    def far_first(i):
        xx = lax.rem(x + 6 + offset(lax.rem(i, 4)), 4)
        yy = lax.rem(y + 12 + offset(lax.div(i, 4)), LINE)
        return LINE * xx + yy

    barrier = pltpu.get_barrier_semaphore()

    def hello_grp(i, carry):
        there = lax.rem(z + GROUPS + offset(GROUPS - 1 - i), GROUPS)
        pl.semaphore_signal(barrier, inc=1, device_id=(there, l), device_id_type=MESH)
        return carry

    lax.fori_loop(0, GROUPS - 1, hello_grp, 0)

    loads = [
        pltpu.make_async_copy(src, dst, load_sem.at[i])
        for i, (src, dst) in enumerate(
            (
                (tok_hbm, tok), (ids_hbm, ids_v), (gw_hbm, gw),
                (wg_hbm.at[0], wg), (wu_hbm.at[0], wu), (wd_hbm.at[0], wd),
            )
        )
    ]
    for copy in loads:
        copy.start()

    def hello_loc(i, carry):
        pl.semaphore_signal(
            barrier, inc=1, device_id=(z, 2 * far_first(i) + c), device_id_type=MESH
        )
        return carry

    lax.fori_loop(0, CHIPS - 1, hello_loc, 0)
    pl.semaphore_signal(barrier, inc=1, device_id=partner, device_id_type=MESH)

    abuf[...] = jnp.zeros(abuf.shape, BF)
    b = iota((BINS, 128), 0)
    n = b >> 4
    half = (n + 1) >> 1
    there = z - jnp.where((n & 1) == 1, half, -half)
    there = jnp.where(there < 0, there + GROUPS, there)
    there = jnp.where(there >= GROUPS, there - GROUPS, there)
    e_b = there * 16 + ((b >> 3) & 1)
    before = onehot(iota((128, 128), 0) < iota((128, 128), 1))
    for copy in loads[:3]:
        copy.wait()
    ids = ids_v[...]
    hit = ids[0:1, :] == e_b
    for k in range(1, 8):
        hit = hit | (ids[k : k + 1, :] == e_b)
    earlier = dot(onehot(hit), before)
    kept = hit & (earlier == (b & 7).astype(F32))
    rows = dot(onehot(kept), tok[...], ((1,), (1,)))
    abuf[:, :, 0:112] = rows.astype(BF).reshape(GROUPS, 16, 112)

    weight = jnp.zeros((BINS, 128), F32)
    for k in range(8):
        weight = jnp.where(ids[k : k + 1, :] == e_b, gw[k : k + 1, :], weight)
    weight = jnp.where(kept, weight, 0.0)
    high = weight.astype(BF)
    wt[0] = high
    wt[1] = (weight - high.astype(F32)).astype(BF)

    i = iota((128, 512), 0)
    n = iota((128, 512), 1)
    match = ((n & 31) < SUB) & (i == (n >> 7) * SUB + (n & 31))
    for r in range(QUAD):
        tmat[128 * r : 128 * (r + 1), :] = onehot(match & (((n >> 5) & 3) == r))

    pl.semaphore_wait(barrier, GROUPS - 1 + CHIPS - 1 + 1)

    for t, (first, fours) in reversed(list(enumerate(CHUNKS))):
        low, high = max(1, 4 * first), 4 * (first + fours)

        def send_a(i, carry, t=t, high=high):
            s = high - 1 - i
            g = lax.rem(z + GROUPS - offset(s), GROUPS)
            send(abuf.at[s], r1.at[s], a_s, a_r.at[t], (g, l))
            return carry

        lax.fori_loop(0, high - low, send_a, 0)
    r1[0] = abuf[0]

    loads[3].wait()
    loads[4].wait()
    i = iota((128, 112), 0)
    widen = onehot(((i & 31) < SUB) & (iota((128, 112), 1) == (i >> 5) * SUB + (i & 31)))
    for m in range(16):
        src, dst = pl.ds(112 * m, 112), pl.ds(128 * m, 128)
        wp[dst, 0:256] = dot(widen, wg[src, :]).astype(BF)
        wp[dst, 256:512] = dot(widen, wu[src, :]).astype(BF)
    loads[5].wait()
    for m in range(16):
        first = 112 * m // 128
        off = 112 * m - 128 * first
        width = 128 if off <= 16 else 256
        i = iota((width, 128), 0)
        n = iota((width, 128), 1)
        spread = onehot(((n & 31) < SUB) & (i == off + (n >> 5) * SUB + (n & 31)))
        dp[:, 128 * m : 128 * (m + 1)] = dot(wd[:, 128 * first : 128 * first + width], spread).astype(BF)

    q = 2 * lax.rem(x, 2) + lax.div(y, 4)

    def mate(k):
        qq = lax.rem(q + k, 4)
        there = LINE * (2 * lax.div(x, 2) + lax.div(qq, 2)) + 4 * lax.rem(qq, 2) + lax.rem(y, 4)
        return (z, 2 * there + c)

    A, PK, F, G, Y, C = range(6)

    def pack(t):
        first, fours = CHUNKS[t]
        pbuf, x2 = chunk_bufs[t][0:2]
        width = 8 * fours
        wait_bytes(r1.at[pl.ds(0, 4 * fours - (1 if first == 0 else 0))], a_r.at[t])
        came = r1[4 * first : 4 * (first + fours)].astype(F32).reshape(fours, QUAD, 16, 128)
        left = [
            jnp.concatenate(
                [came[:, r, 8 * j : 8 * j + 8, :].reshape(width, 128) for r in range(QUAD)], axis=1
            )
            for j in range(2)
        ]
        packed = dot(jnp.concatenate(left, axis=0).astype(BF), tmat[...])
        for j in range(2):
            for qq in range(QUAD):
                pbuf[QUAD * j + qq] = packed[
                    width * j : width * (j + 1), 128 * qq : 128 * (qq + 1)
                ].astype(BF)

        def send_p(i, carry):
            there = far_first(i)
            send(
                pbuf.at[lax.div(there, 4)], x2.at[c, chip], chunk_s.at[t, PK], chunk_r.at[t, PK],
                (z, 2 * there + c),
            )
            return carry

        lax.fori_loop(0, CHIPS - 1, send_p, 0)
        x2[pl.ds(c, 1), pl.ds(chip, 1)] = pbuf[pl.ds(lax.div(chip, 4), 1)].reshape(1, 1, width, 128)

    def forward(t):
        x2 = chunk_bufs[t][1]
        wait_bytes(x2.at[0, pl.ds(0, CHIPS - 1)], chunk_r.at[t, PK])
        send(x2.at[c], x2.at[c], chunk_s.at[t, F], chunk_r.at[t, F], partner)

    def gate_up(t):
        x2, actf, gs, gr = chunk_bufs[t][1:5]
        width = 8 * CHUNKS[t][1]
        wait_bytes(x2.at[0], chunk_r.at[t, F])
        both = [x2[p].astype(F32).reshape(16, 2, width, 128) for p in range(2)]
        w = block_transpose([both[a % 2][:, a // 2].reshape(16 * width, 128) for a in range(4)])
        w = [v.reshape(16, width, 128) for v in w]
        cols = [jnp.concatenate([w[r][m] for r in range(4)], axis=0).astype(BF) for m in range(16)]
        act = dot(jnp.concatenate(cols, axis=1), wp[...])
        actf[...] = act
        gs[...] = act.astype(BF)
        for k in (3, 1, 2):
            send(gs, gr.at[k - 1], chunk_s.at[t, G], chunk_r.at[t, G], mate(k))

    def down(t):
        actf, gs, gr, yb, yr = chunk_bufs[t][2:7]
        width = 8 * CHUNKS[t][1]
        wait_bytes(gr, chunk_r.at[t, G])
        act = actf[...]
        for k in range(3):
            act = act + gr[k].astype(F32)
        gate = act[:, 0:256]
        hidden = (gate * (1.0 / (1.0 + jnp.exp(-gate))) * act[:, 256:512]).astype(BF)
        part = dot(hidden, dp[...])
        w = block_transpose(
            [
                jnp.concatenate(
                    [
                        part[width * r : width * (r + 1), 128 * m : 128 * (m + 1)]
                        for m in range(16)
                    ],
                    axis=0,
                )
                for r in range(4)
            ]
        )
        for a in range(4):
            yb[a % 2, :, a // 2] = w[a].astype(BF).reshape(16, width, 128)
        send(yb.at[other], yr, chunk_s.at[t, Y], chunk_r.at[t, Y], partner)

    def spread_out(t):
        yb, yr, cs, r3 = chunk_bufs[t][5:9]
        width = 8 * CHUNKS[t][1]
        wait_bytes(yr, chunk_r.at[t, Y])
        cs[...] = (yb[c].astype(F32) + yr[...].astype(F32)).astype(BF).reshape(CHIPS, width, 128)

        def send_c(i, carry):
            there = far_first(i)
            send(
                cs.at[there], r3.at[chip], chunk_s.at[t, C], chunk_r.at[t, C], (z, 2 * there + c)
            )
            return carry

        lax.fori_loop(0, CHIPS - 1, send_c, 0)
        r3[pl.ds(chip, 1)] = cs[pl.ds(chip, 1)]

    def home(t):
        first, fours = CHUNKS[t]
        r3 = chunk_bufs[t][8]
        width = 8 * fours
        wait_bytes(r3.at[pl.ds(0, CHIPS - 1)], chunk_r.at[t, C])
        parts = r3[...].astype(F32).reshape(8, 4, width, 128)
        done = parts[:, 0] + parts[:, 1] + parts[:, 2] + parts[:, 3]
        left = [
            jnp.concatenate([done[QUAD * j + qq] for qq in range(QUAD)], axis=1) for j in range(2)
        ]
        laid = dot(jnp.concatenate(left, axis=0).astype(BF), tmat[...], ((1,), (1,)))
        for n in range(fours):
            for r in range(QUAD):
                dbuf[4 * (first + n) + r] = jnp.concatenate(
                    [
                        laid[width * j + 8 * n : width * j + 8 * n + 8, 128 * r : 128 * (r + 1)]
                        for j in range(2)
                    ],
                    axis=0,
                ).astype(BF)
        low, high = max(1, 4 * first), 4 * (first + fours)

        def send_d(i, carry):
            s = high - 1 - i
            send(
                dbuf.at[s], r4.at[s], d_s, d_r, (lax.rem(z + GROUPS + offset(s), GROUPS), l)
            )
            return carry

        lax.fori_loop(0, high - low, send_d, 0)

    count = len(CHUNKS)
    for t in range(count):
        pack(t)
    for t in range(count):
        forward(t)
        if t >= 1:
            gate_up(t - 1)
    gate_up(count - 1)
    for t in range(count):
        down(t)
        if t >= 1:
            spread_out(t - 1)
    spread_out(count - 1)
    for t in reversed(range(count)):
        home(t)
    r4[0] = dbuf[0]
    wait_bytes(r4.at[pl.ds(0, GROUPS - 1)], d_r)
    back = r4[...].reshape(BINS, 128)
    combined = dot(back, wt[0], ((0,), (0,))) + dot(back, wt[1], ((0,), (0,)))
    out_ref[...] = combined[0:112, :].astype(BF)

    wait_bytes(abuf.at[pl.ds(0, GROUPS - 1)], a_s)
    wait_bytes(dbuf.at[pl.ds(0, GROUPS - 1)], d_s)
    for t in range(count):
        x2, gr, yr, cs = (chunk_bufs[t][i] for i in (1, 4, 6, 7))
        wait_bytes(x2.at[0, pl.ds(0, CHIPS - 1)], chunk_s.at[t, PK])
        wait_bytes(x2.at[0], chunk_s.at[t, F])
        wait_bytes(gr, chunk_s.at[t, G])
        wait_bytes(yr, chunk_s.at[t, Y])
        wait_bytes(cs.at[pl.ds(0, CHIPS - 1)], chunk_s.at[t, C])


def chunk_scratch(fours):
    width = 8 * fours
    return [
        pltpu.VMEM((8, width, 128), BF),
        pltpu.VMEM((2, CHIPS, width, 128), BF),
        pltpu.VMEM((4 * width, 512), F32),
        pltpu.VMEM((4 * width, 512), BF),
        pltpu.VMEM((3, 4 * width, 512), BF),
        pltpu.VMEM((2, 16, 2, width, 128), BF),
        pltpu.VMEM((16, 2, width, 128), BF),
        pltpu.VMEM((CHIPS, width, 128), BF),
        pltpu.VMEM((CHIPS, width, 128), BF),
    ]


def shards(tokens, expert_ids, gate_weights, gate_blocks, up_blocks, down_blocks):
    hbm = pl.BlockSpec(memory_space=pl.ANY)
    dma = pltpu.SemaphoreType.DMA
    count = len(CHUNKS)
    combined = pl.pallas_call(
        kernel,
        out_shape=jax.ShapeDtypeStruct(tokens.shape[::-1], BF),
        in_specs=[hbm] * 6,
        out_specs=pl.BlockSpec(memory_space=pltpu.VMEM),
        scratch_shapes=[
            pltpu.VMEM((112, 128), BF),
            pltpu.VMEM((8, 128), jnp.int32),
            pltpu.VMEM((8, 128), F32),
            pltpu.VMEM((1792, 256), BF),
            pltpu.VMEM((1792, 256), BF),
            pltpu.VMEM((256, 1792), BF),
            pltpu.VMEM((2048, 512), BF),
            pltpu.VMEM((256, 2048), BF),
            pltpu.VMEM((512, 512), BF),
            pltpu.VMEM((2, BINS, 128), BF),
            pltpu.VMEM((GROUPS, 16, 128), BF),
            pltpu.VMEM((GROUPS, 16, 128), BF),
            pltpu.VMEM((GROUPS, 16, 128), BF),
            pltpu.VMEM((GROUPS, 16, 128), BF),
            [chunk_scratch(fours) for _, fours in CHUNKS],
            dma((6,)),
            dma, dma((count,)),
            dma, dma,
            dma((count, 6)), dma((count, 6)),
        ],
        compiler_params=pltpu.CompilerParams(
            collective_id=0, has_side_effects=True, vmem_limit_bytes=60 * 1024 * 1024
        ),
        name="moe_layer",
    )(tokens.T, expert_ids.T, gate_weights.T, gate_blocks, up_blocks, down_blocks)
    return combined.T


def solution(mesh):
    in_specs = (
        P("grp", "loc"),
        P("grp", None),
        P("grp", None),
        P(("grp", "loc"), None, None),
        P(("grp", "loc"), None, None),
        P(("grp", "loc"), None, None),
    )
    return jax.shard_map(
        shards, mesh=mesh, in_specs=in_specs, out_specs=P("grp", "loc"), check_vma=False
    )
```

```python
import jax
import jax.numpy as jnp
from jax import lax
from jax.experimental import pallas as pl
from jax.experimental.pallas import tpu as pltpu
from jax.sharding import PartitionSpec as P

MESH = pl.DeviceIdType.MESH
BF = jnp.bfloat16
F32 = jnp.float32

GROUPS = 12
CHIPS = 32
LINE = 8
SUB = 28
QUAD = 4
BINS = GROUPS * 16
CHUNKS = ((0, 1), (1, 1), (2, 1))


def iota(shape, dim):
    return lax.broadcasted_iota(jnp.int32, shape, dim)


def onehot(condition):
    return jnp.where(condition, 1.0, 0.0).astype(BF)


def dot(a, b, dims=((1,), (0,))):
    return lax.dot_general(a, b, (dims, ((), ())), preferred_element_type=F32)


def offset(n):
    return lax.div(n + 1, 2) * (1 - 2 * lax.rem(n + 1, 2))


def block_transpose(v):
    lane = iota(v[0].shape, 1)
    low64 = lane < 64
    low32 = (lane & 32) == 0
    t = [None] * 4
    for a in range(2):
        t[a] = jnp.where(low64, v[a], pltpu.roll(v[a + 2], 64, 1))
        t[a + 2] = jnp.where(low64, pltpu.roll(v[a], 64, 1), v[a + 2])
    w = [None] * 4
    for a in (0, 2):
        w[a] = jnp.where(low32, t[a], pltpu.roll(t[a + 1], 32, 1))
        w[a + 1] = jnp.where(low32, pltpu.roll(t[a], 96, 1), t[a + 1])
    return w


def send(src, dst, send_sem, recv_sem, device):
    pltpu.make_async_remote_copy(
        src_ref=src,
        dst_ref=dst,
        send_sem=send_sem,
        recv_sem=recv_sem,
        device_id=device,
        device_id_type=MESH,
    ).start()


def wait_bytes(ref, sem):
    pltpu.make_async_copy(ref, ref, sem).wait()


def kernel(
    tok_hbm, ids_hbm, gw_hbm, wg_hbm, wu_hbm, wd_hbm, out_ref,
    tok, ids_v, gw, wg, wu, wd, wp, dp, tmat, wt, abuf, r1, dbuf, r4, chunk_bufs,
    load_sem, a_s, a_r, d_s, d_r, chunk_s, chunk_r,
):
    z = lax.axis_index("grp")
    l = lax.axis_index("loc")
    chip = lax.div(l, 2)
    c = lax.rem(l, 2)
    other = 1 - c
    x = lax.div(chip, LINE)
    y = lax.rem(chip, LINE)
    partner = (z, 2 * chip + other)

    def far_first(i):
        xx = lax.rem(x + 6 + offset(lax.rem(i, 4)), 4)
        yy = lax.rem(y + 12 + offset(lax.div(i, 4)), LINE)
        return LINE * xx + yy

    barrier = pltpu.get_barrier_semaphore()

    def hello_grp(i, carry):
        there = lax.rem(z + GROUPS + offset(GROUPS - 1 - i), GROUPS)
        pl.semaphore_signal(barrier, inc=1, device_id=(there, l), device_id_type=MESH)
        return carry

    lax.fori_loop(0, GROUPS - 1, hello_grp, 0)

    loads = [
        pltpu.make_async_copy(src, dst, load_sem.at[i])
        for i, (src, dst) in enumerate(
            (
                (tok_hbm, tok), (ids_hbm, ids_v), (gw_hbm, gw),
                (wg_hbm.at[0], wg), (wu_hbm.at[0], wu), (wd_hbm.at[0], wd),
            )
        )
    ]
    for copy in loads:
        copy.start()

    def hello_loc(i, carry):
        pl.semaphore_signal(
            barrier, inc=1, device_id=(z, 2 * far_first(i) + c), device_id_type=MESH
        )
        return carry

    lax.fori_loop(0, CHIPS - 1, hello_loc, 0)
    pl.semaphore_signal(barrier, inc=1, device_id=partner, device_id_type=MESH)

    abuf[...] = jnp.zeros(abuf.shape, BF)
    b = iota((BINS, 128), 0)
    e_b = (b >> 4) * 16 + ((b >> 3) & 1)
    before = onehot(iota((128, 128), 0) < iota((128, 128), 1))
    for copy in loads[:3]:
        copy.wait()
    ids = ids_v[...]
    hit = ids[0:1, :] == e_b
    for k in range(1, 8):
        hit = hit | (ids[k : k + 1, :] == e_b)
    earlier = dot(onehot(hit), before)
    kept = hit & (earlier == (b & 7).astype(F32))
    rows = dot(onehot(kept), tok[...], ((1,), (1,)))
    abuf[:, :, 0:112] = rows.astype(BF).reshape(GROUPS, 16, 112)

    weight = jnp.zeros((BINS, 128), F32)
    for k in range(8):
        weight = jnp.where(ids[k : k + 1, :] == e_b, gw[k : k + 1, :], weight)
    weight = jnp.where(kept, weight, 0.0)
    high = weight.astype(BF)
    wt[0] = high
    wt[1] = (weight - high.astype(F32)).astype(BF)

    i = iota((128, 512), 0)
    n = iota((128, 512), 1)
    match = ((n & 31) < SUB) & (i == (n >> 7) * SUB + (n & 31))
    for r in range(QUAD):
        tmat[128 * r : 128 * (r + 1), :] = onehot(match & (((n >> 5) & 3) == r))

    pl.semaphore_wait(barrier, GROUPS - 1 + CHIPS - 1 + 1)

    mine = lax.div(z, QUAD)
    pltpu.make_async_copy(abuf.at[z], r1.at[z], a_r.at[mine]).start()

    def send_a(i, carry):
        g = lax.rem(z + GROUPS + offset(GROUPS - 1 - i), GROUPS)
        send(abuf.at[g], r1.at[z], a_s, a_r.at[mine], (g, l))
        return carry

    lax.fori_loop(0, GROUPS - 1, send_a, 0)

    loads[3].wait()
    loads[4].wait()
    i = iota((128, 112), 0)
    widen = onehot(((i & 31) < SUB) & (iota((128, 112), 1) == (i >> 5) * SUB + (i & 31)))
    for m in range(16):
        src, dst = pl.ds(112 * m, 112), pl.ds(128 * m, 128)
        wp[dst, 0:256] = dot(widen, wg[src, :]).astype(BF)
        wp[dst, 256:512] = dot(widen, wu[src, :]).astype(BF)
    loads[5].wait()
    for m in range(16):
        first = 112 * m // 128
        off = 112 * m - 128 * first
        width = 128 if off <= 16 else 256
        i = iota((width, 128), 0)
        n = iota((width, 128), 1)
        spread = onehot(((n & 31) < SUB) & (i == off + (n >> 5) * SUB + (n & 31)))
        dp[:, 128 * m : 128 * (m + 1)] = dot(wd[:, 128 * first : 128 * first + width], spread).astype(BF)

    x_mate = (z, 2 * (chip + LINE * (1 - 2 * lax.rem(x, 2))) + c)
    y_mate = (z, 2 * (LINE * x + lax.rem(y + 4, LINE)) + c)

    PK, F, GX, GY, Y, C = range(6)

    def pack(t):
        first, fours = CHUNKS[t]
        pbuf, x2 = chunk_bufs[t][0:2]
        width = 8 * fours
        wait_bytes(r1.at[pl.ds(4 * first, 4 * fours)], a_r.at[t])
        came = r1[4 * first : 4 * (first + fours)].astype(F32).reshape(fours, QUAD, 16, 128)
        left = [
            jnp.concatenate(
                [came[:, r, 8 * j : 8 * j + 8, :].reshape(width, 128) for r in range(QUAD)], axis=1
            )
            for j in range(2)
        ]
        packed = dot(jnp.concatenate(left, axis=0).astype(BF), tmat[...])
        for j in range(2):
            for qq in range(QUAD):
                pbuf[QUAD * j + qq] = packed[
                    width * j : width * (j + 1), 128 * qq : 128 * (qq + 1)
                ].astype(BF)

        def send_p(i, carry):
            there = far_first(i)
            send(
                pbuf.at[lax.div(there, 4)], x2.at[c, chip], chunk_s.at[t, PK], chunk_r.at[t, PK],
                (z, 2 * there + c),
            )
            return carry

        lax.fori_loop(0, CHIPS - 1, send_p, 0)
        x2[pl.ds(c, 1), pl.ds(chip, 1)] = pbuf[pl.ds(lax.div(chip, 4), 1)].reshape(1, 1, width, 128)

    def forward(t):
        x2 = chunk_bufs[t][1]
        wait_bytes(x2.at[0, pl.ds(0, CHIPS - 1)], chunk_r.at[t, PK])
        send(x2.at[c], x2.at[c], chunk_s.at[t, F], chunk_r.at[t, F], partner)

    def gate_up(t):
        x2, actf, gx, gxr = chunk_bufs[t][1:5]
        width = 8 * CHUNKS[t][1]
        wait_bytes(x2.at[0], chunk_r.at[t, F])
        both = [x2[p].astype(F32).reshape(16, 2, width, 128) for p in range(2)]
        w = block_transpose([both[a % 2][:, a // 2].reshape(16 * width, 128) for a in range(4)])
        w = [v.reshape(16, width, 128) for v in w]
        cols = [jnp.concatenate([w[r][m] for r in range(4)], axis=0).astype(BF) for m in range(16)]
        act = dot(jnp.concatenate(cols, axis=1), wp[...])
        actf[...] = act
        gx[...] = act.astype(BF)
        send(gx, gxr, chunk_s.at[t, GX], chunk_r.at[t, GX], x_mate)

    def gate_up_sum(t):
        actf, gx, gxr, gy, gyr = chunk_bufs[t][2:7]
        wait_bytes(gxr, chunk_r.at[t, GX])
        act = actf[...] + gxr[...].astype(F32)
        actf[...] = act
        gy[...] = act.astype(BF)
        send(gy, gyr, chunk_s.at[t, GY], chunk_r.at[t, GY], y_mate)

    def down(t):
        actf, gx, gxr, gy, gyr, yb, yr = chunk_bufs[t][2:9]
        width = 8 * CHUNKS[t][1]
        wait_bytes(gyr, chunk_r.at[t, GY])
        act = actf[...] + gyr[...].astype(F32)
        gate = act[:, 0:256]
        hidden = (gate * (1.0 / (1.0 + jnp.exp(-gate))) * act[:, 256:512]).astype(BF)
        part = dot(hidden, dp[...])
        w = block_transpose(
            [
                jnp.concatenate(
                    [
                        part[width * r : width * (r + 1), 128 * m : 128 * (m + 1)]
                        for m in range(16)
                    ],
                    axis=0,
                )
                for r in range(4)
            ]
        )
        for a in range(4):
            yb[a % 2, :, a // 2] = w[a].astype(BF).reshape(16, width, 128)
        send(yb.at[other], yr, chunk_s.at[t, Y], chunk_r.at[t, Y], partner)

    def spread_out(t):
        yb, yr, cs, r3 = chunk_bufs[t][7:11]
        width = 8 * CHUNKS[t][1]
        wait_bytes(yr, chunk_r.at[t, Y])
        cs[...] = (yb[c].astype(F32) + yr[...].astype(F32)).astype(BF).reshape(CHIPS, width, 128)

        def send_c(i, carry):
            there = far_first(i)
            send(
                cs.at[there], r3.at[chip], chunk_s.at[t, C], chunk_r.at[t, C], (z, 2 * there + c)
            )
            return carry

        lax.fori_loop(0, CHIPS - 1, send_c, 0)
        r3[pl.ds(chip, 1)] = cs[pl.ds(chip, 1)]

    def home(t):
        first, fours = CHUNKS[t]
        r3 = chunk_bufs[t][10]
        width = 8 * fours
        wait_bytes(r3.at[pl.ds(0, CHIPS - 1)], chunk_r.at[t, C])
        parts = r3[...].astype(F32).reshape(8, 4, width, 128)
        done = parts[:, 0] + parts[:, 1] + parts[:, 2] + parts[:, 3]
        left = [
            jnp.concatenate([done[QUAD * j + qq] for qq in range(QUAD)], axis=1) for j in range(2)
        ]
        laid = dot(jnp.concatenate(left, axis=0).astype(BF), tmat[...], ((1,), (1,)))
        for n in range(fours):
            for r in range(QUAD):
                dbuf[4 * (first + n) + r] = jnp.concatenate(
                    [
                        laid[width * j + 8 * n : width * j + 8 * n + 8, 128 * r : 128 * (r + 1)]
                        for j in range(2)
                    ],
                    axis=0,
                ).astype(BF)
        for n in range(4 * fours):
            group = 4 * first + n

            @pl.when(z == group)
            def _():
                pltpu.make_async_copy(dbuf.at[group], r4.at[group], d_r).start()

            @pl.when(z != group)
            def _():
                send(dbuf.at[group], r4.at[z], d_s, d_r, (group, l))

    for t in range(len(CHUNKS)):
        pack(t)
    forward(0)
    gate_up(0)
    forward(1)
    forward(2)
    gate_up_sum(0)
    gate_up(1)
    gate_up(2)
    gate_up_sum(1)
    gate_up_sum(2)
    down(0)
    spread_out(0)
    down(1)
    down(2)
    spread_out(1)
    spread_out(2)
    home(0)
    home(1)
    home(2)
    wait_bytes(r4, d_r)
    back = r4[...].reshape(BINS, 128)
    combined = dot(back, wt[0], ((0,), (0,))) + dot(back, wt[1], ((0,), (0,)))
    out_ref[...] = combined[0:112, :].astype(BF)

    wait_bytes(abuf.at[pl.ds(0, GROUPS - 1)], a_s)
    wait_bytes(dbuf.at[pl.ds(0, GROUPS - 1)], d_s)
    for t in range(len(CHUNKS)):
        x2, gxr, gyr, yr, cs = (chunk_bufs[t][i] for i in (1, 4, 6, 8, 9))
        wait_bytes(x2.at[0, pl.ds(0, CHIPS - 1)], chunk_s.at[t, PK])
        wait_bytes(x2.at[0], chunk_s.at[t, F])
        wait_bytes(gxr, chunk_s.at[t, GX])
        wait_bytes(gyr, chunk_s.at[t, GY])
        wait_bytes(yr, chunk_s.at[t, Y])
        wait_bytes(cs.at[pl.ds(0, CHIPS - 1)], chunk_s.at[t, C])


def chunk_scratch(fours):
    width = 8 * fours
    return [
        pltpu.VMEM((8, width, 128), BF),
        pltpu.VMEM((2, CHIPS, width, 128), BF),
        pltpu.VMEM((4 * width, 512), F32),
        pltpu.VMEM((4 * width, 512), BF),
        pltpu.VMEM((4 * width, 512), BF),
        pltpu.VMEM((4 * width, 512), BF),
        pltpu.VMEM((4 * width, 512), BF),
        pltpu.VMEM((2, 16, 2, width, 128), BF),
        pltpu.VMEM((16, 2, width, 128), BF),
        pltpu.VMEM((CHIPS, width, 128), BF),
        pltpu.VMEM((CHIPS, width, 128), BF),
    ]


def shards(tokens, expert_ids, gate_weights, gate_blocks, up_blocks, down_blocks):
    hbm = pl.BlockSpec(memory_space=pl.ANY)
    dma = pltpu.SemaphoreType.DMA
    count = len(CHUNKS)
    combined = pl.pallas_call(
        kernel,
        out_shape=jax.ShapeDtypeStruct(tokens.shape[::-1], BF),
        in_specs=[hbm] * 6,
        out_specs=pl.BlockSpec(memory_space=pltpu.VMEM),
        scratch_shapes=[
            pltpu.VMEM((112, 128), BF),
            pltpu.VMEM((8, 128), jnp.int32),
            pltpu.VMEM((8, 128), F32),
            pltpu.VMEM((1792, 256), BF),
            pltpu.VMEM((1792, 256), BF),
            pltpu.VMEM((256, 1792), BF),
            pltpu.VMEM((2048, 512), BF),
            pltpu.VMEM((256, 2048), BF),
            pltpu.VMEM((512, 512), BF),
            pltpu.VMEM((2, BINS, 128), BF),
            pltpu.VMEM((GROUPS, 16, 128), BF),
            pltpu.VMEM((GROUPS, 16, 128), BF),
            pltpu.VMEM((GROUPS, 16, 128), BF),
            pltpu.VMEM((GROUPS, 16, 128), BF),
            [chunk_scratch(fours) for _, fours in CHUNKS],
            dma((6,)),
            dma, dma((count,)),
            dma, dma,
            dma((count, 6)), dma((count, 6)),
        ],
        compiler_params=pltpu.CompilerParams(
            collective_id=0, has_side_effects=True, vmem_limit_bytes=60 * 1024 * 1024
        ),
        name="moe_layer",
    )(tokens.T, expert_ids.T, gate_weights.T, gate_blocks, up_blocks, down_blocks)
    return combined.T


def solution(mesh):
    in_specs = (
        P("grp", "loc"),
        P("grp", None),
        P("grp", None),
        P(("grp", "loc"), None, None),
        P(("grp", "loc"), None, None),
        P(("grp", "loc"), None, None),
    )
    return jax.shard_map(
        shards, mesh=mesh, in_specs=in_specs, out_specs=P("grp", "loc"), check_vma=False
    )
```

```python
import jax
import jax.numpy as jnp
from jax import lax
from jax.experimental import pallas as pl
from jax.experimental.pallas import tpu as pltpu
from jax.sharding import PartitionSpec as P

MESH = pl.DeviceIdType.MESH
BF = jnp.bfloat16
F32 = jnp.float32

GROUPS = 12
CHIPS = 32
LINE = 8
SUB = 28
QUAD = 4
BINS = GROUPS * 16
CHUNKS = ((0, 1), (1, 1), (2, 1))
ONE_STEP = (0,)


def iota(shape, dim):
    return lax.broadcasted_iota(jnp.int32, shape, dim)


def onehot(condition):
    return jnp.where(condition, 1.0, 0.0).astype(BF)


def dot(a, b, dims=((1,), (0,))):
    return lax.dot_general(a, b, (dims, ((), ())), preferred_element_type=F32)


def offset(n):
    return lax.div(n + 1, 2) * (1 - 2 * lax.rem(n + 1, 2))


def block_transpose(v):
    lane = iota(v[0].shape, 1)
    low64 = lane < 64
    low32 = (lane & 32) == 0
    t = [None] * 4
    for a in range(2):
        t[a] = jnp.where(low64, v[a], pltpu.roll(v[a + 2], 64, 1))
        t[a + 2] = jnp.where(low64, pltpu.roll(v[a], 64, 1), v[a + 2])
    w = [None] * 4
    for a in (0, 2):
        w[a] = jnp.where(low32, t[a], pltpu.roll(t[a + 1], 32, 1))
        w[a + 1] = jnp.where(low32, pltpu.roll(t[a], 96, 1), t[a + 1])
    return w


def send(src, dst, send_sem, recv_sem, device):
    pltpu.make_async_remote_copy(
        src_ref=src,
        dst_ref=dst,
        send_sem=send_sem,
        recv_sem=recv_sem,
        device_id=device,
        device_id_type=MESH,
    ).start()


def wait_bytes(ref, sem):
    pltpu.make_async_copy(ref, ref, sem).wait()


def kernel(
    tok_hbm, ids_hbm, gw_hbm, wg_hbm, wu_hbm, wd_hbm, out_ref,
    tok, ids_v, gw, wg, wu, wd, wp, dp, tmat, wt, abuf, r1, dbuf, r4, chunk_bufs,
    load_sem, a_s, a_r, d_s, d_r, chunk_s, chunk_r,
):
    z = lax.axis_index("grp")
    l = lax.axis_index("loc")
    chip = lax.div(l, 2)
    c = lax.rem(l, 2)
    other = 1 - c
    x = lax.div(chip, LINE)
    y = lax.rem(chip, LINE)
    partner = (z, 2 * chip + other)

    def far_first(i):
        xx = lax.rem(x + 6 + offset(lax.rem(i, 4)), 4)
        yy = lax.rem(y + 12 + offset(lax.div(i, 4)), LINE)
        return LINE * xx + yy

    barrier = pltpu.get_barrier_semaphore()

    def hello_grp(i, carry):
        there = lax.rem(z + GROUPS + offset(GROUPS - 1 - i), GROUPS)
        pl.semaphore_signal(barrier, inc=1, device_id=(there, l), device_id_type=MESH)
        return carry

    lax.fori_loop(0, GROUPS - 1, hello_grp, 0)

    loads = [
        pltpu.make_async_copy(src, dst, load_sem.at[i])
        for i, (src, dst) in enumerate(
            (
                (tok_hbm, tok), (ids_hbm, ids_v), (gw_hbm, gw),
                (wg_hbm.at[0], wg), (wu_hbm.at[0], wu), (wd_hbm.at[0], wd),
            )
        )
    ]
    for copy in loads:
        copy.start()

    def hello_loc(i, carry):
        pl.semaphore_signal(
            barrier, inc=1, device_id=(z, 2 * far_first(i) + c), device_id_type=MESH
        )
        return carry

    lax.fori_loop(0, CHIPS - 1, hello_loc, 0)
    pl.semaphore_signal(barrier, inc=1, device_id=partner, device_id_type=MESH)

    abuf[...] = jnp.zeros(abuf.shape, BF)
    b = iota((BINS, 128), 0)
    e_b = (b >> 4) * 16 + ((b >> 3) & 1)
    before = onehot(iota((128, 128), 0) < iota((128, 128), 1))
    for copy in loads[:3]:
        copy.wait()
    ids = ids_v[...]
    hit = ids[0:1, :] == e_b
    for k in range(1, 8):
        hit = hit | (ids[k : k + 1, :] == e_b)
    earlier = dot(onehot(hit), before)
    kept = hit & (earlier == (b & 7).astype(F32))
    rows = dot(onehot(kept), tok[...], ((1,), (1,)))
    abuf[:, :, 0:112] = rows.astype(BF).reshape(GROUPS, 16, 112)

    weight = jnp.zeros((BINS, 128), F32)
    for k in range(8):
        weight = jnp.where(ids[k : k + 1, :] == e_b, gw[k : k + 1, :], weight)
    weight = jnp.where(kept, weight, 0.0)
    high = weight.astype(BF)
    wt[0] = high
    wt[1] = (weight - high.astype(F32)).astype(BF)

    i = iota((128, 512), 0)
    n = iota((128, 512), 1)
    match = ((n & 31) < SUB) & (i == (n >> 7) * SUB + (n & 31))
    for r in range(QUAD):
        tmat[128 * r : 128 * (r + 1), :] = onehot(match & (((n >> 5) & 3) == r))

    pl.semaphore_wait(barrier, GROUPS - 1 + CHIPS - 1 + 1)

    mine = lax.div(z, QUAD)
    pltpu.make_async_copy(abuf.at[z], r1.at[z], a_r.at[mine]).start()

    def send_a(i, carry):
        g = lax.rem(z + GROUPS + offset(GROUPS - 1 - i), GROUPS)
        send(abuf.at[g], r1.at[z], a_s, a_r.at[mine], (g, l))
        return carry

    lax.fori_loop(0, GROUPS - 1, send_a, 0)

    loads[3].wait()
    loads[4].wait()
    i = iota((128, 112), 0)
    widen = onehot(((i & 31) < SUB) & (iota((128, 112), 1) == (i >> 5) * SUB + (i & 31)))
    for m in range(16):
        src, dst = pl.ds(112 * m, 112), pl.ds(128 * m, 128)
        wp[dst, 0:256] = dot(widen, wg[src, :]).astype(BF)
        wp[dst, 256:512] = dot(widen, wu[src, :]).astype(BF)
    loads[5].wait()
    for m in range(16):
        first = 112 * m // 128
        off = 112 * m - 128 * first
        width = 128 if off <= 16 else 256
        i = iota((width, 128), 0)
        n = iota((width, 128), 1)
        spread = onehot(((n & 31) < SUB) & (i == off + (n >> 5) * SUB + (n & 31)))
        dp[:, 128 * m : 128 * (m + 1)] = dot(wd[:, 128 * first : 128 * first + width], spread).astype(BF)

    x_mate = (z, 2 * (chip + LINE * (1 - 2 * lax.rem(x, 2))) + c)
    xy_mate = (z, 2 * (LINE * (x + 1 - 2 * lax.rem(x, 2)) + lax.rem(y + 4, LINE)) + c)
    y_mate = (z, 2 * (LINE * x + lax.rem(y + 4, LINE)) + c)

    PK, F, GX, GY, Y, C = range(6)

    def pack(t):
        first, fours = CHUNKS[t]
        pbuf, x2 = chunk_bufs[t][0:2]
        width = 8 * fours
        wait_bytes(r1.at[pl.ds(4 * first, 4 * fours)], a_r.at[t])
        came = r1[4 * first : 4 * (first + fours)].astype(F32).reshape(fours, QUAD, 16, 128)
        left = [
            jnp.concatenate(
                [came[:, r, 8 * j : 8 * j + 8, :].reshape(width, 128) for r in range(QUAD)], axis=1
            )
            for j in range(2)
        ]
        packed = dot(jnp.concatenate(left, axis=0).astype(BF), tmat[...])
        for j in range(2):
            for qq in range(QUAD):
                pbuf[QUAD * j + qq] = packed[
                    width * j : width * (j + 1), 128 * qq : 128 * (qq + 1)
                ].astype(BF)

        def send_p(i, carry):
            there = far_first(i)
            send(
                pbuf.at[lax.div(there, 4)], x2.at[c, chip], chunk_s.at[t, PK], chunk_r.at[t, PK],
                (z, 2 * there + c),
            )
            return carry

        lax.fori_loop(0, CHIPS - 1, send_p, 0)
        x2[pl.ds(c, 1), pl.ds(chip, 1)] = pbuf[pl.ds(lax.div(chip, 4), 1)].reshape(1, 1, width, 128)

    def forward(t):
        x2 = chunk_bufs[t][1]
        wait_bytes(x2.at[0, pl.ds(0, CHIPS - 1)], chunk_r.at[t, PK])
        send(x2.at[c], x2.at[c], chunk_s.at[t, F], chunk_r.at[t, F], partner)

    def gate_up(t):
        x2, actf, gx, gxr = chunk_bufs[t][1:5]
        width = 8 * CHUNKS[t][1]
        wait_bytes(x2.at[0], chunk_r.at[t, F])
        both = [x2[p].astype(F32).reshape(16, 2, width, 128) for p in range(2)]
        w = block_transpose([both[a % 2][:, a // 2].reshape(16 * width, 128) for a in range(4)])
        w = [v.reshape(16, width, 128) for v in w]
        cols = [jnp.concatenate([w[r][m] for r in range(4)], axis=0).astype(BF) for m in range(16)]
        act = dot(jnp.concatenate(cols, axis=1), wp[...])
        actf[...] = act
        gx[...] = act.astype(BF)
        if t in ONE_STEP:
            gr = chunk_bufs[t][11]
            for k, there in enumerate((xy_mate, y_mate, x_mate)):
                send(gx, gr.at[k], chunk_s.at[t, GX], chunk_r.at[t, GX], there)
            return
        send(gx, gxr, chunk_s.at[t, GX], chunk_r.at[t, GX], x_mate)

    def gate_up_sum(t):
        if t in ONE_STEP:
            return
        actf, gx, gxr, gy, gyr = chunk_bufs[t][2:7]
        wait_bytes(gxr, chunk_r.at[t, GX])
        act = actf[...] + gxr[...].astype(F32)
        actf[...] = act
        gy[...] = act.astype(BF)
        send(gy, gyr, chunk_s.at[t, GY], chunk_r.at[t, GY], y_mate)

    def down(t):
        actf, gx, gxr, gy, gyr, yb, yr = chunk_bufs[t][2:9]
        width = 8 * CHUNKS[t][1]
        if t in ONE_STEP:
            gr = chunk_bufs[t][11]
            wait_bytes(gr, chunk_r.at[t, GX])
            act = (actf[...] + gr[2].astype(F32)) + (gr[1].astype(F32) + gr[0].astype(F32))
        else:
            wait_bytes(gyr, chunk_r.at[t, GY])
            act = actf[...] + gyr[...].astype(F32)
        gate = act[:, 0:256]
        hidden = (gate * (1.0 / (1.0 + jnp.exp(-gate))) * act[:, 256:512]).astype(BF)
        part = dot(hidden, dp[...])
        w = block_transpose(
            [
                jnp.concatenate(
                    [
                        part[width * r : width * (r + 1), 128 * m : 128 * (m + 1)]
                        for m in range(16)
                    ],
                    axis=0,
                )
                for r in range(4)
            ]
        )
        for a in range(4):
            yb[a % 2, :, a // 2] = w[a].reshape(16, width, 128)
        send(yb.at[other], yr, chunk_s.at[t, Y], chunk_r.at[t, Y], partner)

    def spread_out(t):
        yb, yr, cs, r3 = chunk_bufs[t][7:11]
        width = 8 * CHUNKS[t][1]
        wait_bytes(yr, chunk_r.at[t, Y])
        cs[...] = (yb[c] + yr[...]).astype(BF).reshape(CHIPS, width, 128)

        def send_c(i, carry):
            there = far_first(i)
            send(
                cs.at[there], r3.at[chip], chunk_s.at[t, C], chunk_r.at[t, C], (z, 2 * there + c)
            )
            return carry

        lax.fori_loop(0, CHIPS - 1, send_c, 0)
        r3[pl.ds(chip, 1)] = cs[pl.ds(chip, 1)]

    def home(t):
        first, fours = CHUNKS[t]
        r3 = chunk_bufs[t][10]
        width = 8 * fours
        wait_bytes(r3.at[pl.ds(0, CHIPS - 1)], chunk_r.at[t, C])
        parts = r3[...].astype(F32).reshape(8, 4, width, 128)
        done = parts[:, 0] + parts[:, 1] + parts[:, 2] + parts[:, 3]
        left = [
            jnp.concatenate([done[QUAD * j + qq] for qq in range(QUAD)], axis=1) for j in range(2)
        ]
        laid = dot(jnp.concatenate(left, axis=0).astype(BF), tmat[...], ((1,), (1,)))
        for n in range(fours):
            for r in range(QUAD):
                dbuf[4 * (first + n) + r] = jnp.concatenate(
                    [
                        laid[width * j + 8 * n : width * j + 8 * n + 8, 128 * r : 128 * (r + 1)]
                        for j in range(2)
                    ],
                    axis=0,
                ).astype(BF)
        for n in range(4 * fours):
            group = 4 * first + n

            @pl.when(z == group)
            def _():
                pltpu.make_async_copy(dbuf.at[group], r4.at[group], d_r).start()

            @pl.when(z != group)
            def _():
                send(dbuf.at[group], r4.at[z], d_s, d_r, (group, l))

    for t in range(len(CHUNKS)):
        pack(t)
    forward(0)
    gate_up(0)
    forward(1)
    forward(2)
    gate_up_sum(0)
    gate_up(1)
    gate_up(2)
    gate_up_sum(1)
    gate_up_sum(2)
    down(0)
    spread_out(0)
    down(1)
    down(2)
    spread_out(1)
    spread_out(2)
    home(0)
    home(1)
    home(2)
    wait_bytes(abuf.at[pl.ds(0, GROUPS - 1)], a_s)
    for t in range(len(CHUNKS)):
        x2, gxr, gyr, yr, cs = (chunk_bufs[t][i] for i in (1, 4, 6, 8, 9))
        wait_bytes(x2.at[0, pl.ds(0, CHIPS - 1)], chunk_s.at[t, PK])
        wait_bytes(x2.at[0], chunk_s.at[t, F])
        if t in ONE_STEP:
            wait_bytes(chunk_bufs[t][11], chunk_s.at[t, GX])
        else:
            wait_bytes(gxr, chunk_s.at[t, GX])
            wait_bytes(gyr, chunk_s.at[t, GY])
        wait_bytes(yr, chunk_s.at[t, Y])
        wait_bytes(cs.at[pl.ds(0, CHIPS - 1)], chunk_s.at[t, C])
    wait_bytes(r4, d_r)
    back = r4[...].reshape(BINS, 128)
    combined = dot(back, wt[0], ((0,), (0,))) + dot(back, wt[1], ((0,), (0,)))
    out_ref[...] = combined[0:112, :].astype(BF)
    wait_bytes(dbuf.at[pl.ds(0, GROUPS - 1)], d_s)


def chunk_scratch(fours):
    width = 8 * fours
    return [
        pltpu.VMEM((8, width, 128), BF),
        pltpu.VMEM((2, CHIPS, width, 128), BF),
        pltpu.VMEM((4 * width, 512), F32),
        pltpu.VMEM((4 * width, 512), BF),
        pltpu.VMEM((4 * width, 512), BF),
        pltpu.VMEM((4 * width, 512), BF),
        pltpu.VMEM((4 * width, 512), BF),
        pltpu.VMEM((2, 16, 2, width, 128), F32),
        pltpu.VMEM((16, 2, width, 128), F32),
        pltpu.VMEM((CHIPS, width, 128), BF),
        pltpu.VMEM((CHIPS, width, 128), BF),
        pltpu.VMEM((3, 4 * width, 512), BF),
    ]


def shards(tokens, expert_ids, gate_weights, gate_blocks, up_blocks, down_blocks):
    hbm = pl.BlockSpec(memory_space=pl.ANY)
    dma = pltpu.SemaphoreType.DMA
    count = len(CHUNKS)
    combined = pl.pallas_call(
        kernel,
        out_shape=jax.ShapeDtypeStruct(tokens.shape[::-1], BF),
        in_specs=[hbm] * 6,
        out_specs=pl.BlockSpec(memory_space=pltpu.VMEM),
        scratch_shapes=[
            pltpu.VMEM((112, 128), BF),
            pltpu.VMEM((8, 128), jnp.int32),
            pltpu.VMEM((8, 128), F32),
            pltpu.VMEM((1792, 256), BF),
            pltpu.VMEM((1792, 256), BF),
            pltpu.VMEM((256, 1792), BF),
            pltpu.VMEM((2048, 512), BF),
            pltpu.VMEM((256, 2048), BF),
            pltpu.VMEM((512, 512), BF),
            pltpu.VMEM((2, BINS, 128), BF),
            pltpu.VMEM((GROUPS, 16, 128), BF),
            pltpu.VMEM((GROUPS, 16, 128), BF),
            pltpu.VMEM((GROUPS, 16, 128), BF),
            pltpu.VMEM((GROUPS, 16, 128), BF),
            [chunk_scratch(fours) for _, fours in CHUNKS],
            dma((6,)),
            dma, dma((count,)),
            dma, dma,
            dma((count, 6)), dma((count, 6)),
        ],
        compiler_params=pltpu.CompilerParams(
            collective_id=0, has_side_effects=True, vmem_limit_bytes=60 * 1024 * 1024
        ),
        name="moe_layer",
    )(tokens.T, expert_ids.T, gate_weights.T, gate_blocks, up_blocks, down_blocks)
    return combined.T


def solution(mesh):
    in_specs = (
        P("grp", "loc"),
        P("grp", None),
        P("grp", None),
        P(("grp", "loc"), None, None),
        P(("grp", "loc"), None, None),
        P(("grp", "loc"), None, None),
    )
    return jax.shard_map(
        shards, mesh=mesh, in_specs=in_specs, out_specs=P("grp", "loc"), check_vma=False
    )
```

```python
import jax
import jax.numpy as jnp
from jax import lax
from jax.experimental import pallas as pl
from jax.experimental.pallas import tpu as pltpu
from jax.sharding import PartitionSpec as P

MESH = pl.DeviceIdType.MESH
BF = jnp.bfloat16
F32 = jnp.float32

GROUPS = 12
CHIPS = 32
LINE = 8
SUB = 28
QUAD = 4
BINS = GROUPS * 16
CHUNKS = ((0, 1), (1, 1), (2, 1))
ONE_STEP = (0, 1)


def iota(shape, dim):
    return lax.broadcasted_iota(jnp.int32, shape, dim)


def onehot(condition):
    return jnp.where(condition, 1.0, 0.0).astype(BF)


def dot(a, b, dims=((1,), (0,))):
    return lax.dot_general(a, b, (dims, ((), ())), preferred_element_type=F32)


def offset(n):
    return lax.div(n + 1, 2) * (1 - 2 * lax.rem(n + 1, 2))


def block_transpose(v):
    lane = iota(v[0].shape, 1)
    low64 = lane < 64
    low32 = (lane & 32) == 0
    t = [None] * 4
    for a in range(2):
        t[a] = jnp.where(low64, v[a], pltpu.roll(v[a + 2], 64, 1))
        t[a + 2] = jnp.where(low64, pltpu.roll(v[a], 64, 1), v[a + 2])
    w = [None] * 4
    for a in (0, 2):
        w[a] = jnp.where(low32, t[a], pltpu.roll(t[a + 1], 32, 1))
        w[a + 1] = jnp.where(low32, pltpu.roll(t[a], 96, 1), t[a + 1])
    return w


def send(src, dst, send_sem, recv_sem, device):
    pltpu.make_async_remote_copy(
        src_ref=src,
        dst_ref=dst,
        send_sem=send_sem,
        recv_sem=recv_sem,
        device_id=device,
        device_id_type=MESH,
    ).start()


def wait_bytes(ref, sem):
    pltpu.make_async_copy(ref, ref, sem).wait()


def kernel(
    tok_hbm, ids_hbm, gw_hbm, wg_hbm, wu_hbm, wd_hbm, out_ref,
    tok, ids_v, gw, wg, wu, wd, wp, dp, tmat, wt, abuf, r1, dbuf, r4, chunk_bufs,
    load_sem, a_s, a_r, d_s, d_r, chunk_s, chunk_r,
):
    z = lax.axis_index("grp")
    l = lax.axis_index("loc")
    chip = lax.div(l, 2)
    c = lax.rem(l, 2)
    other = 1 - c
    x = lax.div(chip, LINE)
    y = lax.rem(chip, LINE)
    partner = (z, 2 * chip + other)

    def far_first(i):
        xx = lax.rem(x + 6 + offset(lax.rem(i, 4)), 4)
        yy = lax.rem(y + 12 + offset(lax.div(i, 4)), LINE)
        return LINE * xx + yy

    barrier = pltpu.get_barrier_semaphore()

    def hello_grp(i, carry):
        there = lax.rem(z + GROUPS + offset(GROUPS - 1 - i), GROUPS)
        pl.semaphore_signal(barrier, inc=1, device_id=(there, l), device_id_type=MESH)
        return carry

    lax.fori_loop(0, GROUPS - 1, hello_grp, 0)

    loads = [
        pltpu.make_async_copy(src, dst, load_sem.at[i])
        for i, (src, dst) in enumerate(
            (
                (tok_hbm, tok), (ids_hbm, ids_v), (gw_hbm, gw),
                (wg_hbm.at[0], wg), (wu_hbm.at[0], wu), (wd_hbm.at[0], wd),
            )
        )
    ]
    for copy in loads:
        copy.start()

    def hello_loc(i, carry):
        pl.semaphore_signal(
            barrier, inc=1, device_id=(z, 2 * far_first(i) + c), device_id_type=MESH
        )
        return carry

    lax.fori_loop(0, CHIPS - 1, hello_loc, 0)
    pl.semaphore_signal(barrier, inc=1, device_id=partner, device_id_type=MESH)

    abuf[...] = jnp.zeros(abuf.shape, BF)
    b = iota((BINS, 128), 0)
    e_b = (b >> 4) * 16 + ((b >> 3) & 1)
    before = onehot(iota((128, 128), 0) < iota((128, 128), 1))
    for copy in loads[:3]:
        copy.wait()
    ids = ids_v[...]
    hit = ids[0:1, :] == e_b
    for k in range(1, 8):
        hit = hit | (ids[k : k + 1, :] == e_b)
    earlier = dot(onehot(hit), before)
    kept = hit & (earlier == (b & 7).astype(F32))
    rows = dot(onehot(kept), tok[...], ((1,), (1,)))
    abuf[:, :, 0:112] = rows.astype(BF).reshape(GROUPS, 16, 112)

    weight = jnp.zeros((BINS, 128), F32)
    for k in range(8):
        weight = jnp.where(ids[k : k + 1, :] == e_b, gw[k : k + 1, :], weight)
    weight = jnp.where(kept, weight, 0.0)
    high = weight.astype(BF)
    wt[0] = high
    wt[1] = (weight - high.astype(F32)).astype(BF)

    i = iota((128, 512), 0)
    n = iota((128, 512), 1)
    match = ((n & 31) < SUB) & (i == (n >> 7) * SUB + (n & 31))
    for r in range(QUAD):
        tmat[128 * r : 128 * (r + 1), :] = onehot(match & (((n >> 5) & 3) == r))

    pl.semaphore_wait(barrier, GROUPS - 1 + CHIPS - 1 + 1)

    mine = lax.div(z, QUAD)
    pltpu.make_async_copy(abuf.at[z], r1.at[z], a_r.at[mine]).start()

    def send_a(i, carry):
        g = lax.rem(z + GROUPS + offset(GROUPS - 1 - i), GROUPS)
        send(abuf.at[g], r1.at[z], a_s, a_r.at[mine], (g, l))
        return carry

    lax.fori_loop(0, GROUPS - 1, send_a, 0)

    loads[3].wait()
    loads[4].wait()
    i = iota((128, 112), 0)
    widen = onehot(((i & 31) < SUB) & (iota((128, 112), 1) == (i >> 5) * SUB + (i & 31)))
    for m in range(16):
        src, dst = pl.ds(112 * m, 112), pl.ds(128 * m, 128)
        wp[dst, 0:256] = dot(widen, wg[src, :]).astype(BF)
        wp[dst, 256:512] = dot(widen, wu[src, :]).astype(BF)
    loads[5].wait()
    for m in range(16):
        first = 112 * m // 128
        off = 112 * m - 128 * first
        width = 128 if off <= 16 else 256
        i = iota((width, 128), 0)
        n = iota((width, 128), 1)
        spread = onehot(((n & 31) < SUB) & (i == off + (n >> 5) * SUB + (n & 31)))
        dp[:, 128 * m : 128 * (m + 1)] = dot(wd[:, 128 * first : 128 * first + width], spread).astype(BF)

    x_mate = (z, 2 * (chip + LINE * (1 - 2 * lax.rem(x, 2))) + c)
    xy_mate = (z, 2 * (LINE * (x + 1 - 2 * lax.rem(x, 2)) + lax.rem(y + 4, LINE)) + c)
    y_mate = (z, 2 * (LINE * x + lax.rem(y + 4, LINE)) + c)

    PK, F, GX, GY, Y, C = range(6)

    def pack(t):
        first, fours = CHUNKS[t]
        pbuf, x2 = chunk_bufs[t][0:2]
        width = 8 * fours
        wait_bytes(r1.at[pl.ds(4 * first, 4 * fours)], a_r.at[t])
        came = r1[4 * first : 4 * (first + fours)].astype(F32).reshape(fours, QUAD, 16, 128)
        left = [
            jnp.concatenate(
                [came[:, r, 8 * j : 8 * j + 8, :].reshape(width, 128) for r in range(QUAD)], axis=1
            )
            for j in range(2)
        ]
        packed = dot(jnp.concatenate(left, axis=0).astype(BF), tmat[...])
        for j in range(2):
            for qq in range(QUAD):
                pbuf[QUAD * j + qq] = packed[
                    width * j : width * (j + 1), 128 * qq : 128 * (qq + 1)
                ].astype(BF)

        def send_p(i, carry):
            there = far_first(i)
            send(
                pbuf.at[lax.div(there, 4)], x2.at[c, chip], chunk_s.at[t, PK], chunk_r.at[t, PK],
                (z, 2 * there + c),
            )
            return carry

        lax.fori_loop(0, CHIPS - 1, send_p, 0)
        x2[pl.ds(c, 1), pl.ds(chip, 1)] = pbuf[pl.ds(lax.div(chip, 4), 1)].reshape(1, 1, width, 128)

    def forward(t):
        x2 = chunk_bufs[t][1]
        wait_bytes(x2.at[0, pl.ds(0, CHIPS - 1)], chunk_r.at[t, PK])
        send(x2.at[c], x2.at[c], chunk_s.at[t, F], chunk_r.at[t, F], partner)

    def gate_up(t):
        x2, actf, gx, gxr = chunk_bufs[t][1:5]
        width = 8 * CHUNKS[t][1]
        wait_bytes(x2.at[0], chunk_r.at[t, F])
        both = [x2[p].astype(F32).reshape(16, 2, width, 128) for p in range(2)]
        w = block_transpose([both[a % 2][:, a // 2].reshape(16 * width, 128) for a in range(4)])
        w = [v.reshape(16, width, 128) for v in w]
        cols = [jnp.concatenate([w[r][m] for r in range(4)], axis=0).astype(BF) for m in range(16)]
        act = dot(jnp.concatenate(cols, axis=1), wp[...])
        actf[...] = act
        gx[...] = act.astype(BF)
        if t in ONE_STEP:
            gr = chunk_bufs[t][11]
            for k, there in enumerate((xy_mate, y_mate, x_mate)):
                send(gx, gr.at[k], chunk_s.at[t, GX], chunk_r.at[t, GX], there)
            return
        send(gx, gxr, chunk_s.at[t, GX], chunk_r.at[t, GX], x_mate)

    def gate_up_sum(t):
        if t in ONE_STEP:
            return
        actf, gx, gxr, gy, gyr = chunk_bufs[t][2:7]
        wait_bytes(gxr, chunk_r.at[t, GX])
        act = actf[...] + gxr[...].astype(F32)
        actf[...] = act
        gy[...] = act.astype(BF)
        send(gy, gyr, chunk_s.at[t, GY], chunk_r.at[t, GY], y_mate)

    def down(t):
        actf, gx, gxr, gy, gyr, yb, yr = chunk_bufs[t][2:9]
        width = 8 * CHUNKS[t][1]
        if t in ONE_STEP:
            gr = chunk_bufs[t][11]
            wait_bytes(gr, chunk_r.at[t, GX])
            act = (actf[...] + gr[2].astype(F32)) + (gr[1].astype(F32) + gr[0].astype(F32))
        else:
            wait_bytes(gyr, chunk_r.at[t, GY])
            act = actf[...] + gyr[...].astype(F32)
        gate = act[:, 0:256]
        hidden = (gate * (1.0 / (1.0 + jnp.exp(-gate))) * act[:, 256:512]).astype(BF)
        part = dot(hidden, dp[...])
        w = block_transpose(
            [
                jnp.concatenate(
                    [
                        part[width * r : width * (r + 1), 128 * m : 128 * (m + 1)]
                        for m in range(16)
                    ],
                    axis=0,
                )
                for r in range(4)
            ]
        )
        for a in range(4):
            yb[a % 2, :, a // 2] = w[a].reshape(16, width, 128)
        send(yb.at[other], yr, chunk_s.at[t, Y], chunk_r.at[t, Y], partner)

    def spread_out(t):
        yb, yr, cs, r3 = chunk_bufs[t][7:11]
        width = 8 * CHUNKS[t][1]
        wait_bytes(yr, chunk_r.at[t, Y])
        cs[...] = (yb[c] + yr[...]).astype(BF).reshape(CHIPS, width, 128)

        def send_c(i, carry):
            there = far_first(i)
            send(
                cs.at[there], r3.at[chip], chunk_s.at[t, C], chunk_r.at[t, C], (z, 2 * there + c)
            )
            return carry

        lax.fori_loop(0, CHIPS - 1, send_c, 0)
        r3[pl.ds(chip, 1)] = cs[pl.ds(chip, 1)]

    def home(t):
        first, fours = CHUNKS[t]
        r3 = chunk_bufs[t][10]
        width = 8 * fours
        wait_bytes(r3.at[pl.ds(0, CHIPS - 1)], chunk_r.at[t, C])
        parts = r3[...].astype(F32).reshape(8, 4, width, 128)
        done = parts[:, 0] + parts[:, 1] + parts[:, 2] + parts[:, 3]
        left = [
            jnp.concatenate([done[QUAD * j + qq] for qq in range(QUAD)], axis=1) for j in range(2)
        ]
        laid = dot(jnp.concatenate(left, axis=0).astype(BF), tmat[...], ((1,), (1,)))
        for n in range(fours):
            for r in range(QUAD):
                dbuf[4 * (first + n) + r] = jnp.concatenate(
                    [
                        laid[width * j + 8 * n : width * j + 8 * n + 8, 128 * r : 128 * (r + 1)]
                        for j in range(2)
                    ],
                    axis=0,
                ).astype(BF)
        for n in range(4 * fours):
            group = 4 * first + n

            @pl.when(z == group)
            def _():
                pltpu.make_async_copy(dbuf.at[group], r4.at[group], d_r).start()

            @pl.when(z != group)
            def _():
                send(dbuf.at[group], r4.at[z], d_s, d_r, (group, l))

    for t in range(len(CHUNKS)):
        pack(t)
    forward(0)
    gate_up(0)
    forward(1)
    forward(2)
    gate_up_sum(0)
    gate_up(1)
    gate_up(2)
    gate_up_sum(1)
    gate_up_sum(2)
    down(0)
    spread_out(0)
    down(1)
    down(2)
    spread_out(1)
    spread_out(2)
    home(0)
    home(1)
    home(2)
    wait_bytes(abuf.at[pl.ds(0, GROUPS - 1)], a_s)
    for t in range(len(CHUNKS)):
        x2, gxr, gyr, yr, cs = (chunk_bufs[t][i] for i in (1, 4, 6, 8, 9))
        wait_bytes(x2.at[0, pl.ds(0, CHIPS - 1)], chunk_s.at[t, PK])
        wait_bytes(x2.at[0], chunk_s.at[t, F])
        if t in ONE_STEP:
            wait_bytes(chunk_bufs[t][11], chunk_s.at[t, GX])
        else:
            wait_bytes(gxr, chunk_s.at[t, GX])
            wait_bytes(gyr, chunk_s.at[t, GY])
        wait_bytes(yr, chunk_s.at[t, Y])
        wait_bytes(cs.at[pl.ds(0, CHIPS - 1)], chunk_s.at[t, C])
    wait_bytes(r4, d_r)
    back = r4[...].reshape(BINS, 128)
    combined = dot(back, wt[0], ((0,), (0,))) + dot(back, wt[1], ((0,), (0,)))
    out_ref[...] = combined[0:112, :].astype(BF)
    wait_bytes(dbuf.at[pl.ds(0, GROUPS - 1)], d_s)


def chunk_scratch(fours):
    width = 8 * fours
    return [
        pltpu.VMEM((8, width, 128), BF),
        pltpu.VMEM((2, CHIPS, width, 128), BF),
        pltpu.VMEM((4 * width, 512), F32),
        pltpu.VMEM((4 * width, 512), BF),
        pltpu.VMEM((4 * width, 512), BF),
        pltpu.VMEM((4 * width, 512), BF),
        pltpu.VMEM((4 * width, 512), BF),
        pltpu.VMEM((2, 16, 2, width, 128), F32),
        pltpu.VMEM((16, 2, width, 128), F32),
        pltpu.VMEM((CHIPS, width, 128), BF),
        pltpu.VMEM((CHIPS, width, 128), BF),
        pltpu.VMEM((3, 4 * width, 512), BF),
    ]


def shards(tokens, expert_ids, gate_weights, gate_blocks, up_blocks, down_blocks):
    hbm = pl.BlockSpec(memory_space=pl.ANY)
    dma = pltpu.SemaphoreType.DMA
    count = len(CHUNKS)
    combined = pl.pallas_call(
        kernel,
        out_shape=jax.ShapeDtypeStruct(tokens.shape[::-1], BF),
        in_specs=[hbm] * 6,
        out_specs=pl.BlockSpec(memory_space=pltpu.VMEM),
        scratch_shapes=[
            pltpu.VMEM((112, 128), BF),
            pltpu.VMEM((8, 128), jnp.int32),
            pltpu.VMEM((8, 128), F32),
            pltpu.VMEM((1792, 256), BF),
            pltpu.VMEM((1792, 256), BF),
            pltpu.VMEM((256, 1792), BF),
            pltpu.VMEM((2048, 512), BF),
            pltpu.VMEM((256, 2048), BF),
            pltpu.VMEM((512, 512), BF),
            pltpu.VMEM((2, BINS, 128), BF),
            pltpu.VMEM((GROUPS, 16, 128), BF),
            pltpu.VMEM((GROUPS, 16, 128), BF),
            pltpu.VMEM((GROUPS, 16, 128), BF),
            pltpu.VMEM((GROUPS, 16, 128), BF),
            [chunk_scratch(fours) for _, fours in CHUNKS],
            dma((6,)),
            dma, dma((count,)),
            dma, dma,
            dma((count, 6)), dma((count, 6)),
        ],
        compiler_params=pltpu.CompilerParams(
            collective_id=0, has_side_effects=True, vmem_limit_bytes=60 * 1024 * 1024
        ),
        name="moe_layer",
    )(tokens.T, expert_ids.T, gate_weights.T, gate_blocks, up_blocks, down_blocks)
    return combined.T


def solution(mesh):
    in_specs = (
        P("grp", "loc"),
        P("grp", None),
        P("grp", None),
        P(("grp", "loc"), None, None),
        P(("grp", "loc"), None, None),
        P(("grp", "loc"), None, None),
    )
    return jax.shard_map(
        shards, mesh=mesh, in_specs=in_specs, out_specs=P("grp", "loc"), check_vma=False
    )
```
